256 devices in a mesh: tm: 32 (over y, z), row: 2 (over x_lo), col: 4 (over x_hi, core).
Axes of the slice: x: 4 (x_hi: 2, x_lo: 2; x = x_hi * 2 + x_lo), y: 4, z: 8, core: 2. Of those that a mesh axis runs over, the one named last changes fastest.
Arguments:
- latent: bfloat16 [32, 90, 64, 256], P('tm', 'row', 'col'), may hold values from -6 to 6
- conv1_weight: bfloat16 [3, 3, 3, 256, 256], replicated, may hold values from -0.078125 to 0.078125
- conv1_bias: float32 [256], replicated, may hold values from -3 to 3
- conv2_weight: bfloat16 [3, 3, 3, 256, 256], replicated, may hold values from -0.078125 to 0.078125
- conv2_bias: float32 [256], replicated, may hold values from -3 to 3
Outputs:
- mixed: bfloat16 [32, 90, 64, 256], P('tm', 'row', 'col')
The draws below stay inside these ranges and needn't reach their ends.
All inputs are finite; a program needn't handle non-finite values.
Results may differ from the reference program's by a relative error of at most 0.0032.
Values may be sent and summed in bfloat16 or wider, within the bound.
No kernel may reach another device: no remote copies, remote signals or barrier semaphores. Data moves between devices by JAX's collectives and lax.ppermute only.
A program may use at most 64 MiB of HBM per device.

```python
import jax
import jax.numpy as jnp
from jax import lax

CH = 256
FRAMES = 32
HEIGHT = 90
WIDTH = 64


def block_scale(own_key, extent, pieces, least, top_value):
    loudness, own = 1.0, jax.random.fold_in(own_key, 6)
    for position, blocks in pieces:
        draws = jnp.exp(jax.random.uniform(jax.random.fold_in(own, position), (blocks,), jnp.float32, least / len(pieces), top_value / len(pieces)))
        loudness = loudness * jnp.repeat(draws, extent[position] // blocks).reshape([-1 if axis == position else 1 for axis in range(len(extent))])
    return loudness


def bell_draw(rng, extent, width, reach, pieces=(), held_as=jnp.bfloat16):
    gain = block_scale(rng, extent, pieces, -0.22, 0.18) if pieces else 1.0
    values = jax.random.normal(rng, extent, jnp.float32) * width * gain
    return jnp.minimum(jnp.maximum(values, -reach), reach).astype(held_as)


def setup_inputs(seed: int = 0) -> dict:
    seeds = jax.random.split(jax.random.key(seed), 6)
    latent = bell_draw(seeds[0], (FRAMES, HEIGHT, WIDTH, CH), 1.0, 6.0, ((0, 32), (1, 2), (2, 4)))
    conv1_weight = bell_draw(seeds[1], (3, 3, 3, CH, CH), (27 * CH) ** -0.5, 0.078125)
    conv1_bias = bell_draw(seeds[2], (CH,), 0.5, 3.0, (), jnp.float32)
    conv2_weight = bell_draw(seeds[3], (3, 3, 3, CH, CH), (27 * CH) ** -0.5, 0.078125)
    conv2_bias = bell_draw(seeds[4], (CH,), 0.5, 3.0, (), jnp.float32)
    return {"latent": latent, "conv1_weight": conv1_weight, "conv1_bias": conv1_bias, "conv2_weight": conv2_weight, "conv2_bias": conv2_bias}


def convolve(frames, weight, bias):
    in_channels = weight.shape[3]
    out_channels = weight.shape[4]
    taps = weight.reshape(3, 3, 3 * in_channels, out_channels)
    out_rows = frames[0].shape[0] - 2
    out_cols = frames[0].shape[1] - 2
    total = jnp.zeros((out_rows * out_cols, out_channels), jnp.float32)
    for tap_time in range(3):
        for tap_row in range(3):
            band = frames[tap_time][tap_row:tap_row + out_rows]
            joined = jnp.concatenate([band[:, tap_col:tap_col + out_cols] for tap_col in range(3)], axis=-1)
            joined = joined.reshape(out_rows * out_cols, 3 * in_channels)
            total = total + jnp.dot(joined, taps[tap_time, tap_row], preferred_element_type=jnp.float32)
    return (total + bias).reshape(out_rows, out_cols, out_channels)


def layer(active, weight, bias):
    padded = jnp.pad(active, ((2, 0), (1, 1), (1, 1), (0, 0)), mode="edge")

    def one_frame(frame_index):
        frames = tuple(lax.dynamic_index_in_dim(padded, frame_index + offset, 0, keepdims=False) for offset in range(3))
        return convolve(frames, weight, bias)

    return lax.map(one_frame, jnp.arange(active.shape[0], dtype=jnp.int32))


def reference(latent, conv1_weight, conv1_bias, conv2_weight, conv2_bias):
    active = jax.nn.silu(latent.astype(jnp.float32)).astype(jnp.bfloat16)
    hidden = jax.nn.silu(layer(active, conv1_weight, conv1_bias)).astype(jnp.bfloat16)
    result = layer(hidden, conv2_weight, conv2_bias)
    return (latent.astype(jnp.float32) + result).astype(jnp.bfloat16)
```

```python
import functools

import jax
import jax.numpy as jnp
from jax import lax
from jax.experimental import pallas as pl
from jax.experimental.pallas import tpu as pltpu
from jax.sharding import PartitionSpec as P

RING = 8
CH = 256
ROWS, COLS = 45, 16
WIDE = 32
PR = ROWS + 3
HR = ROWS + 1
MAIN = HR * COLS
SIDE = PR
ACC = MAIN + 2 * SIDE
BF, F32 = jnp.bfloat16, jnp.float32


def shifted(count, steps):
    return [(i, (i + steps) % count) for i in range(count)]


def backward_place(source, steps, count):
    block, place = divmod(source, RING)
    if place >= steps:
        return ((block + 1) * RING + place - steps) % count
    return block * RING + place + RING - steps


def backward(count, done, steps):
    return [
        (
            backward_place(i, done, count) if done else i,
            backward_place(i, done + steps, count),
        )
        for i in range(count)
    ]


def silu(v):
    return v / (1.0 + jnp.exp(-v))


def rounded(v):
    return v.astype(BF).astype(F32)


def take(work, start, size, stride=None):
    return jnp.concatenate([work[h, pl.ds(start, size, stride), :] for h in range(2)], axis=1)


def put(work, start, size, value, stride=None):
    for h in range(2):
        work[h, pl.ds(start, size, stride), :] = value[:, h * 128 : (h + 1) * 128]


def pack_kernel(meta, main, halo, out_core, out_far, work):
    row, col = meta[1], meta[2]
    first = 1 + row
    for r in range(ROWS):
        put(work, pl.multiple_of((first + r) * COLS, COLS), COLS, main[pl.ds(r * COLS, COLS), :].astype(F32))
    place = jnp.where(row == 0, ROWS + 1, 0)
    put(work, pl.multiple_of(place * COLS, COLS), 2 * COLS, halo[...].astype(F32))
    src = jnp.where(row == 0, 1, ROWS + 1)
    dst = jnp.where(row == 0, 0, ROWS + 2)
    edge = take(work, pl.multiple_of(src * COLS, COLS), COLS)
    put(work, pl.multiple_of(dst * COLS, COLS), COLS, edge)
    even = lax.rem(col, 2) == 0
    for i in range(2):
        left = take(work, i, PR, COLS)
        right = take(work, COLS - 2 + i, PR, COLS)
        out_core[pl.ds(i * PR, PR), :] = jnp.where(even, right, left).astype(BF)
        out_far[pl.ds(i * PR, PR), :] = jnp.where(even, left, right).astype(BF)


def shift_columns(work, x, rows):
    for r in range(rows):
        for kw in range(3):
            x[kw, pl.ds(r * COLS, COLS), :] = take(work, r * WIDE + 7 + kw, COLS).astype(BF)


def build_frame(meta, main, strips, work, edge, x, side):
    row, col = meta[1], meta[2]
    first = 1 + row
    for r in range(ROWS):
        v = rounded(silu(main[pl.ds(r * COLS, COLS), :].astype(F32)))
        put(work, pl.multiple_of((first + r) * WIDE + 8, 8), COLS, v)
    place = jnp.where(row == 0, ROWS + 1, 0)
    for r in range(2):
        v = rounded(silu(strips[pl.ds(r * COLS, COLS), :].astype(F32)))
        put(work, pl.multiple_of((place + r) * WIDE + 8, 8), COLS, v)
    src = jnp.where(row == 0, 1, ROWS + 1)
    dst = jnp.where(row == 0, 0, ROWS + 2)
    copied = take(work, pl.multiple_of(src * WIDE + 8, 8), COLS)
    put(work, pl.multiple_of(dst * WIDE + 8, 8), COLS, copied)
    even = lax.rem(col, 2) == 0
    west = take(work, 8, PR, WIDE)
    east = take(work, 8 + COLS - 1, PR, WIDE)
    for i in range(2):
        near = rounded(silu(strips[pl.ds(2 * COLS + i * PR, PR), :].astype(F32)))
        far = rounded(silu(strips[pl.ds(2 * COLS + (2 + i) * PR, PR), :].astype(F32)))
        left = jnp.where(col == 0, west, jnp.where(even, far, near))
        right = jnp.where(col == 3, east, jnp.where(even, near, far))
        put(work, 6 + i, PR, left, WIDE)
        put(work, 8 + COLS + i, PR, right, WIDE)
        edge[i, pl.ds(0, PR), :] = left
        edge[4 + i, pl.ds(0, PR), :] = right
    edge[2, pl.ds(0, PR), :] = west
    edge[3, pl.ds(0, PR), :] = east
    for c in range(6):
        edge[c, pl.ds(PR, 8), :] = jnp.zeros((8, CH), F32)
    shift_columns(work, x, PR)
    for kh in range(3):
        for s in range(2):
            for kw in range(3):
                side[kh, kw, pl.ds(s * SIDE, SIDE), :] = edge[3 * s + kw, pl.ds(kh, SIDE), :].astype(BF)


def first_taps(x, side, weight, acc, fresh):
    for kh in range(3):
        for kw in range(3):
            cells = jnp.concatenate([x[kw, pl.ds(kh * COLS, MAIN), :], side[kh, kw]], axis=0)
            part = jnp.dot(cells, weight[0, kh, kw], preferred_element_type=F32)
            if fresh and kh == 0 and kw == 0:
                acc[...] = part
            else:
                acc[...] += part


def second_taps(x, weight, acc, fresh):
    for kh in range(3):
        for kw in range(3):
            part = jnp.dot(
                x[kw, pl.ds(kh * COLS, ROWS * COLS), :],
                weight[0, kh, kw],
                preferred_element_type=F32,
            )
            if fresh and kh == 0 and kw == 0:
                acc[...] = part
            else:
                acc[...] += part


def build_hidden(meta, acc, bias, work, x):
    row, col = meta[1], meta[2]
    first = 1 - row
    b = bias[...]
    for r in range(HR):
        v = rounded(silu(acc[pl.ds(r * COLS, COLS), :] + b))
        put(work, pl.multiple_of((first + r) * WIDE + 8, 8), COLS, v)
    left = rounded(silu(acc[pl.ds(MAIN, HR), :] + b))
    right = rounded(silu(acc[pl.ds(MAIN + SIDE, HR), :] + b))
    for edge_row, start in ((0, 1), (1, 0)):

        @pl.when(row == edge_row)
        def _():
            west = take(work, start * WIDE + 8, HR, WIDE)
            east = take(work, start * WIDE + 8 + COLS - 1, HR, WIDE)
            put(work, start * WIDE + 7, HR, jnp.where(col == 0, west, left), WIDE)
            put(work, start * WIDE + 8 + COLS, HR, jnp.where(col == 3, east, right), WIDE)
            src = 1 if edge_row == 0 else HR - 1
            dst = 0 if edge_row == 0 else HR
            put(work, dst * WIDE, WIDE, take(work, src * WIDE, WIDE))

    shift_columns(work, x, HR + 1)


def kernel_own(meta, main, strips, w1c, h0, work, edge, x, side):
    build_frame(meta, main, strips, work, edge, x, side)
    first_taps(x, side, w1c, h0, True)


def kernel_one(meta, main, strips, w1b, w1c, h0_in, h0, h1, work, edge, x, side):
    build_frame(meta, main, strips, work, edge, x, side)
    h0[...] = h0_in[...]
    first_taps(x, side, w1b, h0, False)
    first_taps(x, side, w1c, h1, True)


def kernel_two(
    meta, main, strips, w1a, w1b, w1c, w2c, bias, h0_in, h1_in, h1, h2, total, work, edge, x, side, h0
):
    build_frame(meta, main, strips, work, edge, x, side)
    h0[...] = h0_in[...]
    first_taps(x, side, w1a, h0, False)
    h1[...] = h1_in[...]
    first_taps(x, side, w1b, h1, False)
    first_taps(x, side, w1c, h2, True)
    build_hidden(meta, h0, bias, work, x)
    second_taps(x, w2c, total, True)


def kernel_three(
    meta, main, strips, w1a, w1b, w2b, bias, h1_in, h2_in, total_in, h2, total, work, edge, x, side, h1
):
    build_frame(meta, main, strips, work, edge, x, side)
    h1[...] = h1_in[...]
    first_taps(x, side, w1a, h1, False)
    h2[...] = h2_in[...]
    first_taps(x, side, w1b, h2, False)
    build_hidden(meta, h1, bias, work, x)
    total[...] = total_in[...]
    second_taps(x, w2b, total, False)


def kernel_four(
    meta, main, strips, w1a, w2a, bias, bias2, h2_in, total_in, latent, out, work, edge, x, side, h2, total
):
    build_frame(meta, main, strips, work, edge, x, side)
    h2[...] = h2_in[...]
    first_taps(x, side, w1a, h2, False)
    build_hidden(meta, h2, bias, work, x)
    total[...] = total_in[...]
    second_taps(x, w2a, total, False)
    out[...] = (latent[...].astype(F32) + (total[...] + bias2[...])).astype(BF)


def whole(shape):
    return pl.BlockSpec(shape, lambda i: (0,) * len(shape), pipeline_mode=pl.Buffered(1))


def tap(kt):
    return pl.BlockSpec(
        (1, 3, 3, CH, CH), lambda i, kt=kt: (kt, 0, 0, 0, 0), pipeline_mode=pl.Buffered(1)
    )


SCRATCH = [
    pltpu.VMEM((2, PR * WIDE, 128), F32),
    pltpu.VMEM((6, PR + 8, CH), F32),
    pltpu.VMEM((3, PR * COLS, CH), BF),
    pltpu.VMEM((3, 3, 2 * SIDE, CH), BF),
]


def run(kernel, operands, taps, outs, scratch, flops, name):
    specs = [pl.BlockSpec(memory_space=pltpu.SMEM)]
    args = []
    for position, operand in enumerate(operands):
        if position:
            kt = taps.get(position)
            specs.append(whole(operand.shape) if kt is None else tap(kt))
        args.append(operand)
    moved = sum(a.size * a.dtype.itemsize for a in args if a.ndim == 2)
    return pl.pallas_call(
        kernel,
        grid=(1,),
        out_shape=outs,
        in_specs=specs,
        out_specs=jax.tree.map(lambda o: whole(o.shape), outs),
        scratch_shapes=scratch,
        compiler_params=pltpu.CompilerParams(vmem_limit_bytes=30 * 2**20),
        cost_estimate=pl.CostEstimate(flops=flops, bytes_accessed=moved, transcendentals=0),
        name=name,
    )(*args)


def local(latent, conv1_weight, conv1_bias, conv2_weight, conv2_bias):
    count = lax.axis_size("tm")
    t = lax.axis_index("tm").astype(jnp.int32)
    row = lax.axis_index("row").astype(jnp.int32)
    col = lax.axis_index("col").astype(jnp.int32)
    meta = jnp.stack([t, row, col])
    own = latent.reshape(ROWS * COLS, CH)
    bias1 = conv1_bias.reshape(1, CH)
    bias2 = conv2_bias.reshape(1, CH)

    ahead = functools.partial(lax.ppermute, axis_name="tm")
    next_frame = shifted(count, 1)
    main1 = ahead(own, perm=next_frame)
    half_way = ahead(own, perm=backward(count, 0, 2))

    to_row = jnp.where(row == 0, own[(ROWS - 2) * COLS :], own[: 2 * COLS])
    rows = lax.ppermute(to_row, "row", [(0, 1), (1, 0)])
    edge_shape = jax.ShapeDtypeStruct((2 * PR, CH), BF)
    to_core, to_far = run(
        pack_kernel, [meta, own, rows], {}, [edge_shape, edge_shape],
        [pltpu.VMEM((2, PR * COLS, 128), F32)], 1000000, "pack",
    )
    near = lax.ppermute(to_core, "col", [(0, 1), (1, 0), (2, 3), (3, 2)])
    far = lax.ppermute(to_far, "col", [(0, 3), (3, 0), (1, 2), (2, 1)])
    strips0 = jnp.concatenate([rows, near, far], axis=0)

    strips1 = ahead(strips0, perm=next_frame)
    strips4 = ahead(strips0, perm=shifted(count, 4))
    main2 = ahead(main1, perm=next_frame)
    strips2 = ahead(strips1, perm=next_frame)
    main4 = ahead(half_way, perm=backward(count, 2, 2))
    main3 = ahead(main2, perm=next_frame)
    strips3 = ahead(strips2, perm=next_frame)

    frames = [(own, strips0)]
    for steps, (m, s) in enumerate(
        ((main1, strips1), (main2, strips2), (main3, strips3), (main4, strips4)), 1
    ):
        m0, s0 = frames[-1]
        frames.append((jnp.where(t >= steps, m, m0), jnp.where(t >= steps, s, s0)))

    hid = jax.ShapeDtypeStruct((ACC, CH), F32)
    tot = jax.ShapeDtypeStruct((ROWS * COLS, CH), F32)
    hid_s = pltpu.VMEM((ACC, CH), F32)
    tot_s = pltpu.VMEM((ROWS * COLS, CH), F32)
    unit = 2 * 9 * ACC * CH * CH
    w1, w2 = conv1_weight, conv2_weight

    h0 = run(kernel_own, [meta, *frames[0], w1], {3: 2}, hid, SCRATCH, unit, "own")
    h0, h1 = run(
        kernel_one, [meta, *frames[1], w1, w1, h0], {3: 1, 4: 2}, [hid, hid], SCRATCH, 2 * unit, "one"
    )
    h1, h2, total = run(
        kernel_two, [meta, *frames[2], w1, w1, w1, w2, bias1, h0, h1],
        {3: 0, 4: 1, 5: 2, 6: 2}, [hid, hid, tot], SCRATCH + [hid_s], 4 * unit, "two",
    )
    h2, total = run(
        kernel_three, [meta, *frames[3], w1, w1, w2, bias1, h1, h2, total],
        {3: 0, 4: 1, 5: 1}, [hid, tot], SCRATCH + [hid_s], 3 * unit, "three",
    )
    out = run(
        kernel_four, [meta, *frames[4], w1, w2, bias1, bias2, h2, total, own],
        {3: 0, 4: 0}, jax.ShapeDtypeStruct((ROWS * COLS, CH), BF), SCRATCH + [hid_s, tot_s],
        2 * unit, "four",
    )
    return out.reshape(1, ROWS, COLS, CH)


def solution(mesh):
    in_specs = (P("tm", "row", "col", None), P(), P(), P(), P())
    out_specs = P("tm", "row", "col", None)
    return jax.shard_map(local, mesh=mesh, in_specs=in_specs, out_specs=out_specs, check_vma=False)
```

```python
import functools

import jax
import jax.numpy as jnp
from jax import lax
from jax.experimental import pallas as pl
from jax.experimental.pallas import tpu as pltpu
from jax.sharding import PartitionSpec as P

RING = 8
CH = 256
ROWS, COLS = 45, 16
LIMIT = 30 * 2**20
COST = (1000000000, 2000000000, 4000000000, 3000000000, 2000000000)
FORTH = (45,)
BACK = (45,)
HALF = 2
WIDE = 32
PR = ROWS + 3
HR = ROWS + 1
MAIN = HR * COLS
SIDE = PR
ACC = MAIN + 2 * SIDE
BF, F32 = jnp.bfloat16, jnp.float32


def shifted(count, steps):
    return [(i, (i + steps) % count) for i in range(count)]


def backward_place(source, steps, count):
    block, place = divmod(source, RING)
    if place >= steps:
        return ((block + 1) * RING + place - steps) % count
    return block * RING + place + RING - steps


def backward(count, done, steps):
    return [
        (
            backward_place(i, done, count) if done else i,
            backward_place(i, done + steps, count),
        )
        for i in range(count)
    ]


def silu(v):
    return (0.5 * v) * (1.0 + jnp.tanh(0.5 * v))


def rounded(v):
    return v.astype(BF).astype(F32)


def take(work, start, size, stride=None):
    return jnp.concatenate([work[h, pl.ds(start, size, stride), :] for h in range(2)], axis=1)


def put(work, start, size, value, stride=None):
    for h in range(2):
        work[h, pl.ds(start, size, stride), :] = value[:, h * 128 : (h + 1) * 128]


def pack_kernel(meta, main, halo, out_core, out_far, work):
    row, col = meta[1], meta[2]
    first = 1 + row
    for r in range(ROWS):
        put(work, pl.multiple_of((first + r) * COLS, COLS), COLS, main[pl.ds(r * COLS, COLS), :].astype(F32))
    place = jnp.where(row == 0, ROWS + 1, 0)
    put(work, pl.multiple_of(place * COLS, COLS), 2 * COLS, halo[...].astype(F32))
    src = jnp.where(row == 0, 1, ROWS + 1)
    dst = jnp.where(row == 0, 0, ROWS + 2)
    edge = take(work, pl.multiple_of(src * COLS, COLS), COLS)
    put(work, pl.multiple_of(dst * COLS, COLS), COLS, edge)
    even = lax.rem(col, 2) == 0
    for i in range(2):
        left = take(work, i, PR, COLS)
        right = take(work, COLS - 2 + i, PR, COLS)
        out_core[pl.ds(i * PR, PR), :] = jnp.where(even, right, left).astype(BF)
        out_far[pl.ds(i * PR, PR), :] = jnp.where(even, left, right).astype(BF)


def shift_columns(work, x, rows):
    for r in range(rows):
        for kw in range(3):
            x[kw, pl.ds(r * COLS, COLS), :] = take(work, r * WIDE + 7 + kw, COLS).astype(BF)


def build_frame(meta, main, strips, work, edge, x, side):
    row, col = meta[1], meta[2]
    first = 1 + row
    for r in range(ROWS):
        v = rounded(silu(main[pl.ds(r * COLS, COLS), :].astype(F32)))
        put(work, pl.multiple_of((first + r) * WIDE + 8, 8), COLS, v)
    place = jnp.where(row == 0, ROWS + 1, 0)
    for r in range(2):
        v = rounded(silu(strips[pl.ds(r * COLS, COLS), :].astype(F32)))
        put(work, pl.multiple_of((place + r) * WIDE + 8, 8), COLS, v)
    src = jnp.where(row == 0, 1, ROWS + 1)
    dst = jnp.where(row == 0, 0, ROWS + 2)
    copied = take(work, pl.multiple_of(src * WIDE + 8, 8), COLS)
    put(work, pl.multiple_of(dst * WIDE + 8, 8), COLS, copied)
    even = lax.rem(col, 2) == 0
    west = take(work, 8, PR, WIDE)
    east = take(work, 8 + COLS - 1, PR, WIDE)
    for i in range(2):
        near = rounded(silu(strips[pl.ds(2 * COLS + i * PR, PR), :].astype(F32)))
        far = rounded(silu(strips[pl.ds(2 * COLS + (2 + i) * PR, PR), :].astype(F32)))
        left = jnp.where(col == 0, west, jnp.where(even, far, near))
        right = jnp.where(col == 3, east, jnp.where(even, near, far))
        put(work, 6 + i, PR, left, WIDE)
        put(work, 8 + COLS + i, PR, right, WIDE)
        edge[i, pl.ds(0, PR), :] = left
        edge[4 + i, pl.ds(0, PR), :] = right
    edge[2, pl.ds(0, PR), :] = west
    edge[3, pl.ds(0, PR), :] = east
    for c in range(6):
        edge[c, pl.ds(PR, 8), :] = jnp.zeros((8, CH), F32)
    shift_columns(work, x, PR)
    for kh in range(3):
        for s in range(2):
            for kw in range(3):
                side[kh, kw, pl.ds(s * SIDE, SIDE), :] = edge[3 * s + kw, pl.ds(kh, SIDE), :].astype(BF)


def first_taps(x, side, weight, carried, out):
    cells = jnp.concatenate(
        [
            jnp.concatenate([x[kw, pl.ds(kh * COLS, MAIN), :], side[kh, kw]], axis=0)
            for kh in range(3)
            for kw in range(3)
        ],
        axis=1,
    )
    part = jnp.dot(cells, weight.reshape(9 * CH, CH), preferred_element_type=F32)
    out[...] = part if carried is None else carried[...] + part


def second_taps(x, weight):
    cells = jnp.concatenate(
        [x[kw, pl.ds(kh * COLS, ROWS * COLS), :] for kh in range(3) for kw in range(3)], axis=1
    )
    return jnp.dot(cells, weight.reshape(9 * CH, CH), preferred_element_type=F32)


def build_hidden(meta, acc, bias, work, x):
    row, col = meta[1], meta[2]
    first = 1 - row
    b = bias
    for r in range(HR):
        v = rounded(silu(acc[pl.ds(r * COLS, COLS), :] + b))
        put(work, pl.multiple_of((first + r) * WIDE + 8, 8), COLS, v)
    left = rounded(silu(acc[pl.ds(MAIN, HR), :] + b))
    right = rounded(silu(acc[pl.ds(MAIN + SIDE, HR), :] + b))
    for edge_row, start in ((0, 1), (1, 0)):

        @pl.when(row == edge_row)
        def _():
            west = take(work, start * WIDE + 8, HR, WIDE)
            east = take(work, start * WIDE + 8 + COLS - 1, HR, WIDE)
            put(work, start * WIDE + 7, HR, jnp.where(col == 0, west, left), WIDE)
            put(work, start * WIDE + 8 + COLS, HR, jnp.where(col == 3, east, right), WIDE)
            src = 1 if edge_row == 0 else HR - 1
            dst = 0 if edge_row == 0 else HR
            put(work, dst * WIDE, WIDE, take(work, src * WIDE, WIDE))

    shift_columns(work, x, HR + 1)


def step_kernel(steps, plan, *refs):
    refs = list(refs)
    pop = lambda count: [refs.pop(0) for _ in range(count)]
    (meta,) = pop(1)
    mains = [pop(count) for count in plan["parts"]]
    strips = [pop(1)[0] if apart else None for apart in plan["apart"]]
    (w1,) = pop(1)
    w2, biases = pop(2) if plan["done"] is not None else (None, None)
    (latent,) = pop(1) if plan["last"] else (None,)
    sums_in = dict(zip(plan["carried"], pop(len(plan["carried"]))))
    total_in = pop(1)[0] if plan["total_in"] else None
    outs = pop(plan["outs"])
    main, strip, work, edge, x, side, ready = refs
    for k in range(steps + 1):

        @pl.when(meta[0] >= steps if k == steps else meta[0] == k)
        def _():
            at = 0
            for part in mains[k]:
                size = min(part.shape[0], ROWS * COLS - at)
                main[pl.ds(at, size), :] = part[pl.ds(0, size), :]
                at += size
            if strips[k] is None:
                strip[...] = part[pl.ds(size, strip.shape[0]), :]
            else:
                strip[...] = strips[k][...]

    build_frame(meta, main, strip, work, edge, x, side)
    kept = [f for f in plan["frames"] if f != plan["done"]]
    for frame in plan["frames"][::-1]:
        out = ready if frame == plan["done"] else outs[kept.index(frame)]
        first_taps(x, side, w1[2 - (steps - frame)], sums_in.get(frame), out)
    if plan["done"] is not None:
        build_hidden(meta, ready, biases[0:1], work, x)
        total = second_taps(x, w2[2 - plan["done"]])
        if total_in is not None:
            total = total_in[...] + total
        if plan["last"]:
            total = (latent[...].astype(F32) + (total + biases[1:2])).astype(BF)
        outs[-1][...] = total


SCRATCH = [
    pltpu.VMEM((ROWS * COLS, CH), BF),
    pltpu.VMEM((2 * COLS + 4 * PR, CH), BF),
    pltpu.VMEM((2, PR * WIDE, 128), F32),
    pltpu.VMEM((6, PR + 8, CH), F32),
    pltpu.VMEM((3, PR * COLS, CH), BF),
    pltpu.VMEM((3, 3, 2 * SIDE, CH), BF),
    pltpu.VMEM((ACC, CH), F32),
]
SMEM = pl.BlockSpec(memory_space=pltpu.SMEM)
VMEM = pl.BlockSpec(memory_space=pltpu.VMEM)


def step(steps, meta, frames, weights, latent, sums, total):
    frames_here = [f for f in range(3) if 0 <= steps - f <= 2]
    done = steps - 2 if steps >= 2 else None
    plan = {
        "frames": frames_here,
        "carried": [f for f in frames_here if f in sums],
        "done": done,
        "last": steps == 4,
        "total_in": total is not None,
    }
    hid = jax.ShapeDtypeStruct((ACC, CH), F32)
    tot = jax.ShapeDtypeStruct((ROWS * COLS, CH), F32)
    kept = [f for f in frames_here if f != done]
    out_shape = [hid] * len(kept)
    if steps == 4:
        out_shape = [jax.ShapeDtypeStruct((ROWS * COLS, CH), BF)]
    elif done is not None:
        out_shape = out_shape + [tot]
    plan["outs"] = len(out_shape)
    mains = [part for f in frames for part in f[0]]
    strips = [f[1] for f in frames if f[1] is not None]
    plan["apart"] = [f[1] is not None for f in frames]
    plan["parts"] = [len(f[0]) for f in frames]
    w1, w2, biases = weights
    args = [meta, *mains, *strips, w1]
    args += [w2, biases] if done is not None else []
    args += [latent] if steps == 4 else []
    args += [sums[f] for f in plan["carried"]] + ([total] if total is not None else [])
    specs = [SMEM] + [VMEM] * (len(args) - 1)
    outs = pl.pallas_call(
        functools.partial(step_kernel, steps, plan),
        out_shape=out_shape,
        in_specs=specs,
        out_specs=[VMEM] * len(out_shape),
        scratch_shapes=SCRATCH,
        compiler_params=pltpu.CompilerParams(vmem_limit_bytes=LIMIT),
        cost_estimate=pl.CostEstimate(
            flops=COST[steps],
            bytes_accessed=1000000,
            transcendentals=0,
        ),
        name="step" + str(steps),
    )(*args)
    if steps == 4:
        return outs[0]
    sums = {f: o for f, o in zip(kept, outs)}
    return sums, (outs[-1] if done is not None else None)


def tie(value, *first):
    return lax.optimization_barrier((value, *first))[0]


def join_kernel(*refs):
    *parts, out = refs
    at = 0
    for part in parts:
        out[pl.ds(at, part.shape[0]), :] = part[...]
        at += part.shape[0]


def join(*parts):
    return pl.pallas_call(
        join_kernel,
        out_shape=jax.ShapeDtypeStruct((sum(p.shape[0] for p in parts), CH), BF),
        in_specs=[VMEM] * len(parts),
        out_specs=VMEM,
        compiler_params=pltpu.CompilerParams(vmem_limit_bytes=LIMIT),
        cost_estimate=pl.CostEstimate(flops=1000000, bytes_accessed=800000, transcendentals=0),
        name="join",
    )(*parts)


def cut_kernel(meta, own, to_row, *parts):
    last = ROWS - 2
    to_row[...] = jnp.where(
        meta[1] == 0, own[pl.ds(last * COLS, 2 * COLS), :], own[pl.ds(0, 2 * COLS), :]
    )
    at = 0
    for part in parts:
        if at == ROWS * COLS:
            at = 0
        part[...] = own[pl.ds(at, part.shape[0]), :]
        at += part.shape[0]


def cut(meta, own, sizes):
    shapes = [jax.ShapeDtypeStruct((r * COLS, CH), BF) for r in (2, *sizes)]
    return pl.pallas_call(
        cut_kernel,
        out_shape=shapes,
        in_specs=[SMEM, VMEM],
        out_specs=[VMEM] * len(shapes),
        compiler_params=pltpu.CompilerParams(vmem_limit_bytes=LIMIT),
        cost_estimate=pl.CostEstimate(flops=1000000, bytes_accessed=800000, transcendentals=0),
        name="cut",
    )(meta, own)


def pack(meta, own, rows):
    edge = jax.ShapeDtypeStruct((2 * PR, CH), BF)
    return pl.pallas_call(
        pack_kernel,
        out_shape=[edge, edge],
        in_specs=[SMEM, VMEM, VMEM],
        out_specs=[VMEM, VMEM],
        scratch_shapes=[pltpu.VMEM((2, PR * COLS, 128), F32)],
        compiler_params=pltpu.CompilerParams(vmem_limit_bytes=LIMIT),
        cost_estimate=pl.CostEstimate(flops=1000000, bytes_accessed=800000, transcendentals=0),
        name="pack",
    )(meta, own, rows)


def local(latent, conv1_weight, conv1_bias, conv2_weight, conv2_bias):
    count = lax.axis_size("tm")
    t = lax.axis_index("tm").astype(jnp.int32)
    row = lax.axis_index("row").astype(jnp.int32)
    col = lax.axis_index("col").astype(jnp.int32)
    meta = jnp.stack([t, row, col])
    own = latent.reshape(ROWS * COLS, CH)
    biases = jnp.stack([conv1_bias, conv2_bias])

    ahead = functools.partial(lax.ppermute, axis_name="tm")
    next_frame = shifted(count, 1)
    to_row = jnp.where(row == 0, own[(ROWS - 2) * COLS :], own[: 2 * COLS])
    rows = lax.ppermute(to_row, "row", [(0, 1), (1, 0)])
    main1 = ahead(own, perm=next_frame)
    half_way = ahead(own, perm=backward(count, 0, HALF))
    to_core, to_far = pack(meta, own, rows)
    near = lax.ppermute(to_core, "col", [(0, 1), (1, 0), (2, 3), (3, 2)])
    far = lax.ppermute(to_far, "col", [(0, 3), (3, 0), (1, 2), (2, 1)])
    strips0 = join(rows, near, far)
    strips1 = ahead(strips0, perm=next_frame)
    strips2 = ahead(strips0, perm=shifted(count, 2))
    strips4 = ahead(strips0, perm=shifted(count, 4))

    main2 = ahead(tie(main1, strips0), perm=next_frame)
    main4 = ahead(half_way, perm=backward(count, HALF, 4 - HALF))
    weights = (conv1_weight, conv2_weight, biases)
    frames = [([own], strips0), ([main1], strips1)]
    sums, total = step(0, meta, frames[:1], weights, own, {}, None)
    main2 = tie(main2, sums[0])
    main3 = ahead(main2, perm=next_frame)
    strips3 = ahead(tie(strips2, sums[0]), perm=next_frame)
    sums, total = step(1, meta, frames, weights, own, sums, total)
    frames += [([main2], strips2), ([main3], strips3), ([main4], strips4)]
    sums, total = step(2, meta, frames[:3], weights, own, sums, total)
    sums, total = step(3, meta, frames[:4], weights, own, sums, total)
    out = step(4, meta, frames, weights, own, sums, total)
    return out.reshape(1, ROWS, COLS, CH)


def solution(mesh):
    in_specs = (P("tm", "row", "col", None), P(), P(), P(), P())
    out_specs = P("tm", "row", "col", None)
    return jax.shard_map(local, mesh=mesh, in_specs=in_specs, out_specs=out_specs, check_vma=False)
```

```python
import functools

import jax
import jax.numpy as jnp
from jax import lax
from jax.experimental import pallas as pl
from jax.experimental.pallas import tpu as pltpu
from jax.sharding import PartitionSpec as P

RING = 8
CH = 256
ROWS, COLS = 45, 16
LIMIT = 30 * 2**20
COST = (1000000000, 2000000000, 4000000000, 3000000000, 2000000000)
FORTH = (45,)
BACK = (45,)
HALF = 2
WIDE = 32
PR = ROWS + 3
HR = ROWS + 1
MAIN = HR * COLS
SIDE = PR
ACC = MAIN + 2 * SIDE
BF, F32 = jnp.bfloat16, jnp.float32


def shifted(count, steps):
    return [(i, (i + steps) % count) for i in range(count)]


def backward_place(source, steps, count):
    block, place = divmod(source, RING)
    early = 0 < steps < 4
    moved = place in ((4, 5, 6) if early else (4, 5, 6, 7)) if steps else False
    return ((block + moved) * RING + (place - steps) % RING) % count


def backward(count, done, steps):
    return [
        (backward_place(i, done, count), backward_place(i, done + steps, count))
        for i in range(count)
    ]


def silu(v):
    return (0.5 * v) * (1.0 + jnp.tanh(0.5 * v))


def rounded(v):
    return v.astype(BF).astype(F32)


def take(work, start, size, stride=None):
    return jnp.concatenate([work[h, pl.ds(start, size, stride), :] for h in range(2)], axis=1)


def put(work, start, size, value, stride=None):
    for h in range(2):
        work[h, pl.ds(start, size, stride), :] = value[:, h * 128 : (h + 1) * 128]


def pack_kernel(meta, main, halo, out_core, out_far, work):
    row, col = meta[1], meta[2]
    first = 1 + row
    for r in range(ROWS):
        put(work, pl.multiple_of((first + r) * COLS, COLS), COLS, main[pl.ds(r * COLS, COLS), :].astype(F32))
    place = jnp.where(row == 0, ROWS + 1, 0)
    put(work, pl.multiple_of(place * COLS, COLS), 2 * COLS, halo[...].astype(F32))
    src = jnp.where(row == 0, 1, ROWS + 1)
    dst = jnp.where(row == 0, 0, ROWS + 2)
    edge = take(work, pl.multiple_of(src * COLS, COLS), COLS)
    put(work, pl.multiple_of(dst * COLS, COLS), COLS, edge)
    even = lax.rem(col, 2) == 0
    for i in range(2):
        left = take(work, i, PR, COLS)
        right = take(work, COLS - 2 + i, PR, COLS)
        out_core[pl.ds(i * PR, PR), :] = jnp.where(even, right, left).astype(BF)
        out_far[pl.ds(i * PR, PR), :] = jnp.where(even, left, right).astype(BF)


def shift_columns(work, x, rows):
    for r in range(rows):
        for kw in range(3):
            x[kw, pl.ds(r * COLS, COLS), :] = take(work, r * WIDE + 7 + kw, COLS).astype(BF)


def build_frame(meta, main, strips, work, edge, x, side):
    row, col = meta[1], meta[2]
    first = 1 + row
    for r in range(ROWS):
        v = rounded(silu(main[pl.ds(r * COLS, COLS), :].astype(F32)))
        put(work, pl.multiple_of((first + r) * WIDE + 8, 8), COLS, v)
    place = jnp.where(row == 0, ROWS + 1, 0)
    for r in range(2):
        v = rounded(silu(strips[pl.ds(r * COLS, COLS), :].astype(F32)))
        put(work, pl.multiple_of((place + r) * WIDE + 8, 8), COLS, v)
    src = jnp.where(row == 0, 1, ROWS + 1)
    dst = jnp.where(row == 0, 0, ROWS + 2)
    copied = take(work, pl.multiple_of(src * WIDE + 8, 8), COLS)
    put(work, pl.multiple_of(dst * WIDE + 8, 8), COLS, copied)
    even = lax.rem(col, 2) == 0
    west = take(work, 8, PR, WIDE)
    east = take(work, 8 + COLS - 1, PR, WIDE)
    for i in range(2):
        near = rounded(silu(strips[pl.ds(2 * COLS + i * PR, PR), :].astype(F32)))
        far = rounded(silu(strips[pl.ds(2 * COLS + (2 + i) * PR, PR), :].astype(F32)))
        left = jnp.where(col == 0, west, jnp.where(even, far, near))
        right = jnp.where(col == 3, east, jnp.where(even, near, far))
        put(work, 6 + i, PR, left, WIDE)
        put(work, 8 + COLS + i, PR, right, WIDE)
        edge[i, pl.ds(0, PR), :] = left
        edge[4 + i, pl.ds(0, PR), :] = right
    edge[2, pl.ds(0, PR), :] = west
    edge[3, pl.ds(0, PR), :] = east
    for c in range(6):
        edge[c, pl.ds(PR, 8), :] = jnp.zeros((8, CH), F32)
    shift_columns(work, x, PR)
    for kh in range(3):
        for s in range(2):
            for kw in range(3):
                side[kh, kw, pl.ds(s * SIDE, SIDE), :] = edge[3 * s + kw, pl.ds(kh, SIDE), :].astype(BF)


def first_taps(x, side, weight, carried, out):
    cells = jnp.concatenate(
        [
            jnp.concatenate([x[kw, pl.ds(kh * COLS, MAIN), :], side[kh, kw]], axis=0)
            for kh in range(3)
            for kw in range(3)
        ],
        axis=1,
    )
    part = jnp.dot(cells, weight.reshape(9 * CH, CH), preferred_element_type=F32)
    out[...] = part if carried is None else carried[...] + part


def second_taps(x, weight):
    cells = jnp.concatenate(
        [x[kw, pl.ds(kh * COLS, ROWS * COLS), :] for kh in range(3) for kw in range(3)], axis=1
    )
    return jnp.dot(cells, weight.reshape(9 * CH, CH), preferred_element_type=F32)


def build_hidden(meta, acc, bias, work, x):
    row, col = meta[1], meta[2]
    first = 1 - row
    b = bias
    for r in range(HR):
        v = rounded(silu(acc[pl.ds(r * COLS, COLS), :] + b))
        put(work, pl.multiple_of((first + r) * WIDE + 8, 8), COLS, v)
    left = rounded(silu(acc[pl.ds(MAIN, HR), :] + b))
    right = rounded(silu(acc[pl.ds(MAIN + SIDE, HR), :] + b))
    for edge_row, start in ((0, 1), (1, 0)):

        @pl.when(row == edge_row)
        def _():
            west = take(work, start * WIDE + 8, HR, WIDE)
            east = take(work, start * WIDE + 8 + COLS - 1, HR, WIDE)
            put(work, start * WIDE + 7, HR, jnp.where(col == 0, west, left), WIDE)
            put(work, start * WIDE + 8 + COLS, HR, jnp.where(col == 3, east, right), WIDE)
            src = 1 if edge_row == 0 else HR - 1
            dst = 0 if edge_row == 0 else HR
            put(work, dst * WIDE, WIDE, take(work, src * WIDE, WIDE))

    shift_columns(work, x, HR + 1)


def step_kernel(steps, plan, *refs):
    refs = list(refs)
    pop = lambda count: [refs.pop(0) for _ in range(count)]
    (meta,) = pop(1)
    mains = [pop(count) for count in plan["parts"]]
    strips = pop(steps + 1 - plan["late"])
    (w1,) = pop(1)
    w2, biases = pop(2) if plan["done"] else (None, None)
    (latent,) = pop(1) if plan["last"] else (None,)
    sums_in = dict(zip(plan["carried"], pop(len(plan["carried"]))))
    total_in = pop(1)[0] if plan["total_in"] else None
    outs = pop(plan["outs"])
    main, strip, work, edge, x, side, ready = refs[:7]
    for k in range(steps + 1):
        if plan["late"] and k == steps - 1:
            continue
        source = k - (plan["late"] and k == steps)

        @pl.when(meta[0] >= steps if k == steps else meta[0] == k)
        def _():
            main[...] = mains[source][0][...]
            strip[...] = strips[source][...]

    def add():
        build_frame(meta, main, strip, work, edge, x, side)
        kept = [f for f in plan["frames"] if f not in plan["done"]]
        for frame in plan["frames"][::-1]:
            if frame in plan["done"]:
                out = ready.at[plan["done"].index(frame)]
            else:
                out = outs[kept.index(frame)]
            first_taps(x, side, w1[2 - (steps - frame)], sums_in.get(frame), out)

    if plan["late"]:
        pl.when(meta[0] != steps - 1)(add)

        @pl.when(meta[0] == steps - 1)
        def _():
            outs[0][...] = sums_in[plan["frames"][0]][...]

    else:
        add()
    if plan["last"]:

        @pl.when(meta[0] == steps)
        def _():
            first_taps(x, side, w1[0], ready.at[1], ready.at[1])

    if plan["done"]:
        total = 0.0 if total_in is None else total_in[...]
        for i, frame in enumerate(plan["done"]):
            room = (work, x) if i == 0 else refs[7:9]
            build_hidden(meta, ready.at[i], biases[0:1], *room)
        for i, frame in enumerate(plan["done"]):
            total = total + second_taps(x if i == 0 else refs[8], w2[2 - frame])
        if plan["last"]:
            total = (latent[...].astype(F32) + (total + biases[1:2])).astype(BF)
        outs[-1][...] = total


SCRATCH = [
    pltpu.VMEM((ROWS * COLS, CH), BF),
    pltpu.VMEM((2 * COLS + 4 * PR, CH), BF),
    pltpu.VMEM((2, PR * WIDE, 128), F32),
    pltpu.VMEM((6, PR + 8, CH), F32),
    pltpu.VMEM((3, PR * COLS, CH), BF),
    pltpu.VMEM((3, 3, 2 * SIDE, CH), BF),
    pltpu.VMEM((2, ACC, CH), F32),
]
SECOND = [
    pltpu.VMEM((2, PR * WIDE, 128), F32),
    pltpu.VMEM((3, PR * COLS, CH), BF),
]
SMEM = pl.BlockSpec(memory_space=pltpu.SMEM)
VMEM = pl.BlockSpec(memory_space=pltpu.VMEM)


def step(steps, meta, frames, weights, latent, sums, total):
    late = steps == 4
    last = steps == 3
    frames_here = [f for f in range(3) if 0 <= steps - f <= 2]
    done = {2: [0], 3: [1, 2]}.get(steps, [])
    if late:
        frames = frames[:3] + frames[4:]
    plan = {
        "frames": frames_here,
        "carried": [f for f in frames_here if f in sums],
        "done": done,
        "last": last,
        "late": late,
        "total_in": total is not None and not late,
    }
    hid = jax.ShapeDtypeStruct((ACC, CH), F32)
    tot = jax.ShapeDtypeStruct((ROWS * COLS, CH), F32)
    kept = [f for f in frames_here if f not in done]
    out_shape = [hid] * len(kept)
    if last:
        out_shape = [jax.ShapeDtypeStruct((ROWS * COLS, CH), BF)]
    elif done:
        out_shape = out_shape + [tot]
    plan["outs"] = len(out_shape)
    mains = [part for f in frames for part in f[0]]
    strips = [f[1] for f in frames if f[1] is not None]
    plan["parts"] = [len(f[0]) for f in frames]
    w1, w2, biases = weights
    args = [meta, *mains, *strips, w1]
    args += [w2, biases] if done else []
    args += [latent] if last else []
    args += [sums[f] for f in plan["carried"]] + ([total] if plan["total_in"] else [])
    specs = [SMEM] + [VMEM] * (len(args) - 1)
    outs = pl.pallas_call(
        functools.partial(step_kernel, steps, plan),
        out_shape=out_shape,
        in_specs=specs,
        out_specs=[VMEM] * len(out_shape),
        scratch_shapes=SCRATCH + (SECOND if last else []),
        compiler_params=pltpu.CompilerParams(vmem_limit_bytes=LIMIT),
        cost_estimate=pl.CostEstimate(
            flops=COST[steps],
            bytes_accessed=1000000,
            transcendentals=0,
        ),
        name="step" + str(steps),
    )(*args)
    if last:
        return outs[0]
    return {**sums, **dict(zip(kept, outs))}, (outs[-1] if done else total)


def tie(value, *first):
    return lax.optimization_barrier((value, *first))[0]


def join_kernel(*refs):
    *parts, out = refs
    at = 0
    for part in parts:
        out[pl.ds(at, part.shape[0]), :] = part[...]
        at += part.shape[0]


def join(*parts):
    return pl.pallas_call(
        join_kernel,
        out_shape=jax.ShapeDtypeStruct((sum(p.shape[0] for p in parts), CH), BF),
        in_specs=[VMEM] * len(parts),
        out_specs=VMEM,
        compiler_params=pltpu.CompilerParams(vmem_limit_bytes=LIMIT),
        cost_estimate=pl.CostEstimate(flops=1000000, bytes_accessed=800000, transcendentals=0),
        name="join",
    )(*parts)


def cut_kernel(meta, own, to_row, *parts):
    last = ROWS - 2
    to_row[...] = jnp.where(
        meta[1] == 0, own[pl.ds(last * COLS, 2 * COLS), :], own[pl.ds(0, 2 * COLS), :]
    )
    at = 0
    for part in parts:
        if at == ROWS * COLS:
            at = 0
        part[...] = own[pl.ds(at, part.shape[0]), :]
        at += part.shape[0]


def cut(meta, own, sizes):
    shapes = [jax.ShapeDtypeStruct((r * COLS, CH), BF) for r in (2, *sizes)]
    return pl.pallas_call(
        cut_kernel,
        out_shape=shapes,
        in_specs=[SMEM, VMEM],
        out_specs=[VMEM] * len(shapes),
        compiler_params=pltpu.CompilerParams(vmem_limit_bytes=LIMIT),
        cost_estimate=pl.CostEstimate(flops=1000000, bytes_accessed=800000, transcendentals=0),
        name="cut",
    )(meta, own)


def pack(meta, own, rows):
    edge = jax.ShapeDtypeStruct((2 * PR, CH), BF)
    return pl.pallas_call(
        pack_kernel,
        out_shape=[edge, edge],
        in_specs=[SMEM, VMEM, VMEM],
        out_specs=[VMEM, VMEM],
        scratch_shapes=[pltpu.VMEM((2, PR * COLS, 128), F32)],
        compiler_params=pltpu.CompilerParams(vmem_limit_bytes=LIMIT),
        cost_estimate=pl.CostEstimate(flops=1000000, bytes_accessed=800000, transcendentals=0),
        name="pack",
    )(meta, own, rows)


def local(latent, conv1_weight, conv1_bias, conv2_weight, conv2_bias):
    count = lax.axis_size("tm")
    t = lax.axis_index("tm").astype(jnp.int32)
    row = lax.axis_index("row").astype(jnp.int32)
    col = lax.axis_index("col").astype(jnp.int32)
    meta = jnp.stack([t, row, col])
    own = latent.reshape(ROWS * COLS, CH)
    biases = jnp.stack([conv1_bias, conv2_bias])

    ahead = functools.partial(lax.ppermute, axis_name="tm")
    next_frame = shifted(count, 1)
    to_row = jnp.where(row == 0, own[(ROWS - 2) * COLS :], own[: 2 * COLS])
    rows = lax.ppermute(to_row, "row", [(0, 1), (1, 0)])
    main1 = ahead(own, perm=next_frame)
    half_way = ahead(own, perm=backward(count, 0, HALF))
    to_core, to_far = pack(meta, own, rows)
    near = lax.ppermute(to_core, "col", [(0, 1), (1, 0), (2, 3), (3, 2)])
    far = lax.ppermute(to_far, "col", [(0, 3), (3, 0), (1, 2), (2, 1)])
    strips0 = join(rows, near, far)
    strips1 = ahead(strips0, perm=next_frame)
    strips2 = ahead(strips0, perm=shifted(count, 2))
    strips4 = ahead(strips0, perm=shifted(count, 4))

    main2 = ahead(tie(main1, to_core), perm=next_frame)
    main4 = ahead(half_way, perm=backward(count, HALF, 4 - HALF))
    weights = (conv1_weight, conv2_weight, biases)
    frames = [([own], strips0), ([main1], strips1)]
    sums, total = step(0, tie(meta, half_way), frames[:1], weights, own, {}, None)
    main2 = tie(main2, sums[0])
    main3 = ahead(main2, perm=next_frame)
    strips3 = ahead(tie(strips2, sums[0]), perm=next_frame)
    sums, total = step(1, meta, frames, weights, own, sums, total)
    frames += [([main2], strips2), ([main3], strips3), ([main4], strips4)]
    sums, total = step(2, meta, frames[:3], weights, own, sums, total)
    sums, total = step(4, meta, frames, weights, own, sums, total)
    out = step(3, meta, frames[:4], weights, own, sums, total)
    return out.reshape(1, ROWS, COLS, CH)


def solution(mesh):
    in_specs = (P("tm", "row", "col", None), P(), P(), P(), P())
    out_specs = P("tm", "row", "col", None)
    return jax.shard_map(local, mesh=mesh, in_specs=in_specs, out_specs=out_specs, check_vma=False)
```

```python
import functools

import jax
import jax.numpy as jnp
from jax import lax
from jax.experimental import pallas as pl
from jax.experimental.pallas import tpu as pltpu
from jax.sharding import PartitionSpec as P

RING = 8
CH = 256
ROWS, COLS = 45, 16
LIMIT = 30 * 2**20
COST = (1000000000, 2000000000, 2000000000, 3000000000, 500000000)
FORTH = (45,)
BACK = (45,)
HALF = 2
WIDE = 32
PR = ROWS + 3
HR = ROWS + 1
MAIN = HR * COLS
SIDE = PR
ACC = MAIN + 2 * SIDE
BF, F32 = jnp.bfloat16, jnp.float32


def shifted(count, steps):
    return [(i, (i + steps) % count) for i in range(count)]


def backward_place(source, steps, count):
    block, place = divmod(source, RING)
    early = 0 < steps < 4
    moved = place in ((4, 5, 6) if early else (4, 5, 6, 7)) if steps else False
    return ((block + moved) * RING + (place - steps) % RING) % count


def backward(count, done, steps):
    return [
        (backward_place(i, done, count), backward_place(i, done + steps, count))
        for i in range(count)
    ]


def silu(v):
    return (0.5 * v) * (1.0 + jnp.tanh(0.5 * v))


def rounded(v):
    return v.astype(BF).astype(F32)


def take(work, start, size, stride=None):
    return jnp.concatenate([work[h, pl.ds(start, size, stride), :] for h in range(2)], axis=1)


def put(work, start, size, value, stride=None):
    for h in range(2):
        work[h, pl.ds(start, size, stride), :] = value[:, h * 128 : (h + 1) * 128]


def pack_kernel(meta, main, halo, out_core, out_far, own, work):
    own[...] = main[...]
    row, col = meta[1], meta[2]
    first = 1 + row
    for r in range(ROWS):
        put(work, pl.multiple_of((first + r) * COLS, COLS), COLS, main[pl.ds(r * COLS, COLS), :].astype(F32))
    place = jnp.where(row == 0, ROWS + 1, 0)
    put(work, pl.multiple_of(place * COLS, COLS), 2 * COLS, halo[...].astype(F32))
    src = jnp.where(row == 0, 1, ROWS + 1)
    dst = jnp.where(row == 0, 0, ROWS + 2)
    edge = take(work, pl.multiple_of(src * COLS, COLS), COLS)
    put(work, pl.multiple_of(dst * COLS, COLS), COLS, edge)
    even = lax.rem(col, 2) == 0
    for i in range(2):
        left = take(work, i, PR, COLS)
        right = take(work, COLS - 2 + i, PR, COLS)
        out_core[pl.ds(i * PR, PR), :] = jnp.where(even, right, left).astype(BF)
        out_far[pl.ds(i * PR, PR), :] = jnp.where(even, left, right).astype(BF)


def shift_columns(work, x, rows):
    for r in range(rows):
        for kw in range(3):
            x[kw, pl.ds(r * COLS, COLS), :] = take(work, r * WIDE + 7 + kw, COLS).astype(BF)


def build_frame(meta, main, strips, work, edge, x, side):
    row, col = meta[1], meta[2]
    first = 1 + row
    for r in range(ROWS):
        v = rounded(silu(main[pl.ds(r * COLS, COLS), :].astype(F32)))
        put(work, pl.multiple_of((first + r) * WIDE + 8, 8), COLS, v)
    place = jnp.where(row == 0, ROWS + 1, 0)
    for r in range(2):
        v = rounded(silu(strips[pl.ds(r * COLS, COLS), :].astype(F32)))
        put(work, pl.multiple_of((place + r) * WIDE + 8, 8), COLS, v)
    src = jnp.where(row == 0, 1, ROWS + 1)
    dst = jnp.where(row == 0, 0, ROWS + 2)
    copied = take(work, pl.multiple_of(src * WIDE + 8, 8), COLS)
    put(work, pl.multiple_of(dst * WIDE + 8, 8), COLS, copied)
    even = lax.rem(col, 2) == 0
    west = take(work, 8, PR, WIDE)
    east = take(work, 8 + COLS - 1, PR, WIDE)
    for i in range(2):
        near = rounded(silu(strips[pl.ds(2 * COLS + i * PR, PR), :].astype(F32)))
        far = rounded(silu(strips[pl.ds(2 * COLS + (2 + i) * PR, PR), :].astype(F32)))
        left = jnp.where(col == 0, west, jnp.where(even, far, near))
        right = jnp.where(col == 3, east, jnp.where(even, near, far))
        put(work, 6 + i, PR, left, WIDE)
        put(work, 8 + COLS + i, PR, right, WIDE)
        edge[i, pl.ds(0, PR), :] = left
        edge[4 + i, pl.ds(0, PR), :] = right
    edge[2, pl.ds(0, PR), :] = west
    edge[3, pl.ds(0, PR), :] = east
    for c in range(6):
        edge[c, pl.ds(PR, 8), :] = jnp.zeros((8, CH), F32)
    shift_columns(work, x, PR)
    for kh in range(3):
        for s in range(2):
            for kw in range(3):
                side[kh, kw, pl.ds(s * SIDE, SIDE), :] = edge[3 * s + kw, pl.ds(kh, SIDE), :].astype(BF)


def first_taps(x, side, weight, carried, out):
    cells = jnp.concatenate(
        [
            jnp.concatenate([x[kw, pl.ds(kh * COLS, MAIN), :], side[kh, kw]], axis=0)
            for kh in range(3)
            for kw in range(3)
        ],
        axis=1,
    )
    part = jnp.dot(cells, weight.reshape(9 * CH, CH), preferred_element_type=F32)
    out[...] = part if carried is None else carried[...] + part


def second_taps(x, weight):
    cells = jnp.concatenate(
        [x[kw, pl.ds(kh * COLS, ROWS * COLS), :] for kh in range(3) for kw in range(3)], axis=1
    )
    return jnp.dot(cells, weight.reshape(9 * CH, CH), preferred_element_type=F32)


def build_hidden(meta, acc, bias, work, x):
    row, col = meta[1], meta[2]
    first = 1 - row
    b = bias
    for r in range(HR):
        v = rounded(silu(acc[pl.ds(r * COLS, COLS), :] + b))
        put(work, pl.multiple_of((first + r) * WIDE + 8, 8), COLS, v)
    left = rounded(silu(acc[pl.ds(MAIN, HR), :] + b))
    right = rounded(silu(acc[pl.ds(MAIN + SIDE, HR), :] + b))
    for edge_row, start in ((0, 1), (1, 0)):

        @pl.when(row == edge_row)
        def _():
            west = take(work, start * WIDE + 8, HR, WIDE)
            east = take(work, start * WIDE + 8 + COLS - 1, HR, WIDE)
            put(work, start * WIDE + 7, HR, jnp.where(col == 0, west, left), WIDE)
            put(work, start * WIDE + 8 + COLS, HR, jnp.where(col == 3, east, right), WIDE)
            src = 1 if edge_row == 0 else HR - 1
            dst = 0 if edge_row == 0 else HR
            put(work, dst * WIDE, WIDE, take(work, src * WIDE, WIDE))

    shift_columns(work, x, HR + 1)


def step_kernel(steps, plan, *refs):
    refs = list(refs)
    pop = lambda count: [refs.pop(0) for _ in range(count)]
    (meta,) = pop(1)
    mains = [pop(count) for count in plan["parts"]]
    strips = pop(steps + 1 - plan["late"])
    (w1,) = pop(1)
    w2, bias1 = pop(2) if plan["done"] else (None, None)
    bias2, latent = pop(2) if plan["last"] else (None, None)
    sums_in = dict(zip(plan["carried"], pop(len(plan["carried"]))))
    total_in = pop(1)[0] if plan["total_in"] else None
    outs = pop(plan["outs"])
    main, strip, work, edge, x, side, ready = refs[:7]
    for k in range(steps + 1):
        if plan["late"] and k == steps - 1:
            continue
        source = k - (plan["late"] and k == steps)

        @pl.when(meta[0] >= steps if k == steps else meta[0] == k)
        def _():
            main[...] = mains[source][0][...]
            strip[...] = strips[source][...]

    def add():
        build_frame(meta, main, strip, work, edge, x, side)
        kept = [f for f in plan["frames"] if f not in plan["done"]]
        for frame in plan["frames"][::-1]:
            if frame in plan["done"]:
                out = ready.at[plan["done"].index(frame)]
            else:
                out = outs[kept.index(frame)]
            first_taps(x, side, w1[2 - (steps - frame)], sums_in.get(frame), out)

    if plan["late"]:
        pl.when(meta[0] != steps - 1)(add)

        @pl.when(meta[0] == steps - 1)
        def _():
            outs[0][...] = sums_in[plan["frames"][0]][...]

    else:
        add()
    if plan["last"]:

        @pl.when(meta[0] == steps)
        def _():
            first_taps(x, side, w1[0], ready.at[1], ready.at[1])

    if plan["done"]:
        total = 0.0 if total_in is None else total_in[...]
        for i, frame in enumerate(plan["done"]):
            room = (work, x) if i == 0 else refs[7:9]
            build_hidden(meta, ready.at[i], bias1[...], *room)
        for i, frame in enumerate(plan["done"]):
            total = total + second_taps(x if i == 0 else refs[8], w2[2 - frame])
        if plan["last"]:
            total = (latent[...].astype(F32) + (total + bias2[...])).astype(BF)
        outs[-1][...] = total


SCRATCH = [
    pltpu.VMEM((ROWS * COLS, CH), BF),
    pltpu.VMEM((2 * COLS + 4 * PR, CH), BF),
    pltpu.VMEM((2, PR * WIDE, 128), F32),
    pltpu.VMEM((6, PR + 8, CH), F32),
    pltpu.VMEM((3, PR * COLS, CH), BF),
    pltpu.VMEM((3, 3, 2 * SIDE, CH), BF),
    pltpu.VMEM((2, ACC, CH), F32),
]
SECOND = [
    pltpu.VMEM((2, PR * WIDE, 128), F32),
    pltpu.VMEM((3, PR * COLS, CH), BF),
]
ANY = pl.BlockSpec(memory_space=pl.ANY)
SMEM = pl.BlockSpec(memory_space=pltpu.SMEM)
VMEM = pl.BlockSpec(memory_space=pltpu.VMEM)


def step(steps, meta, frames, weights, latent, sums, total):
    late = steps == 4
    last = steps == 3
    frames_here = [f for f in range(3) if 0 <= steps - f <= 2]
    done = {2: [0], 3: [1, 2]}.get(steps, [])
    if late:
        frames = frames[:3] + frames[4:]
    plan = {
        "frames": frames_here,
        "carried": [f for f in frames_here if f in sums],
        "done": done,
        "last": last,
        "late": late,
        "total_in": total is not None and not late,
    }
    hid = jax.ShapeDtypeStruct((ACC, CH), F32)
    tot = jax.ShapeDtypeStruct((ROWS * COLS, CH), F32)
    kept = [f for f in frames_here if f not in done]
    out_shape = [hid] * len(kept)
    if last:
        out_shape = [jax.ShapeDtypeStruct((ROWS * COLS, CH), BF)]
    elif done:
        out_shape = out_shape + [tot]
    plan["outs"] = len(out_shape)
    mains = [part for f in frames for part in f[0]]
    strips = [f[1] for f in frames if f[1] is not None]
    plan["parts"] = [len(f[0]) for f in frames]
    w1, w2, biases = weights
    args = [meta, *mains, *strips, w1]
    args += [w2, biases[0]] if done else []
    args += [biases[1], latent] if last else []
    args += [sums[f] for f in plan["carried"]] + ([total] if plan["total_in"] else [])
    specs = [SMEM] + [VMEM] * (len(args) - 1)
    outs = pl.pallas_call(
        functools.partial(step_kernel, steps, plan),
        out_shape=out_shape,
        in_specs=specs,
        out_specs=[VMEM] * len(out_shape),
        scratch_shapes=SCRATCH + (SECOND if last else []),
        compiler_params=pltpu.CompilerParams(vmem_limit_bytes=LIMIT),
        cost_estimate=pl.CostEstimate(
            flops=COST[steps],
            bytes_accessed=1000000,
            transcendentals=0,
        ),
        name="step" + str(steps),
    )(*args)
    if last:
        return outs[0]
    return {**sums, **dict(zip(kept, outs))}, (outs[-1] if done else total)


def bring_kernel(source, target, sem):
    copy = pltpu.make_async_copy(source, target, sem)
    copy.start()
    copy.wait()


def bring(weight):
    return pl.pallas_call(
        bring_kernel,
        out_shape=jax.ShapeDtypeStruct(weight.shape, weight.dtype),
        in_specs=[ANY],
        out_specs=VMEM,
        scratch_shapes=[pltpu.SemaphoreType.DMA],
        compiler_params=pltpu.CompilerParams(vmem_limit_bytes=LIMIT),
        cost_estimate=pl.CostEstimate(flops=1000000000, bytes_accessed=1000, transcendentals=0),
        name="bring",
    )(weight)


def tie(value, *first):
    return lax.optimization_barrier((value, *first))[0]


def join_kernel(*refs):
    *parts, out = refs
    at = 0
    for part in parts:
        out[pl.ds(at, part.shape[0]), :] = part[...]
        at += part.shape[0]


def join(*parts):
    return pl.pallas_call(
        join_kernel,
        out_shape=jax.ShapeDtypeStruct((sum(p.shape[0] for p in parts), CH), BF),
        in_specs=[VMEM] * len(parts),
        out_specs=VMEM,
        compiler_params=pltpu.CompilerParams(vmem_limit_bytes=LIMIT),
        cost_estimate=pl.CostEstimate(flops=1000000, bytes_accessed=800000, transcendentals=0),
        name="join",
    )(*parts)


def cut_kernel(meta, own, to_row, *parts):
    last = ROWS - 2
    to_row[...] = jnp.where(
        meta[1] == 0, own[pl.ds(last * COLS, 2 * COLS), :], own[pl.ds(0, 2 * COLS), :]
    )
    at = 0
    for part in parts:
        if at == ROWS * COLS:
            at = 0
        part[...] = own[pl.ds(at, part.shape[0]), :]
        at += part.shape[0]


def cut(meta, own, sizes):
    shapes = [jax.ShapeDtypeStruct((r * COLS, CH), BF) for r in (2, *sizes)]
    return pl.pallas_call(
        cut_kernel,
        out_shape=shapes,
        in_specs=[SMEM, VMEM],
        out_specs=[VMEM] * len(shapes),
        compiler_params=pltpu.CompilerParams(vmem_limit_bytes=LIMIT),
        cost_estimate=pl.CostEstimate(flops=1000000, bytes_accessed=800000, transcendentals=0),
        name="cut",
    )(meta, own)


def pack(meta, own, rows):
    edge = jax.ShapeDtypeStruct((2 * PR, CH), BF)
    return pl.pallas_call(
        pack_kernel,
        out_shape=[
            edge,
            edge,
            jax.ShapeDtypeStruct((ROWS * COLS, CH), BF),
        ],
        in_specs=[SMEM, VMEM, VMEM],
        out_specs=[VMEM] * 3,
        scratch_shapes=[pltpu.VMEM((2, PR * COLS, 128), F32)],
        compiler_params=pltpu.CompilerParams(vmem_limit_bytes=LIMIT),
        cost_estimate=pl.CostEstimate(flops=1000000, bytes_accessed=800000, transcendentals=0),
        name="pack",
    )(meta, own, rows)


def local(latent, conv1_weight, conv1_bias, conv2_weight, conv2_bias):
    count = lax.axis_size("tm")
    t = lax.axis_index("tm").astype(jnp.int32)
    row = lax.axis_index("row").astype(jnp.int32)
    col = lax.axis_index("col").astype(jnp.int32)
    meta = jnp.stack([t, row, col])
    own = latent.reshape(ROWS * COLS, CH)

    ahead = functools.partial(lax.ppermute, axis_name="tm")
    next_frame = shifted(count, 1)
    to_row = jnp.where(row == 0, own[(ROWS - 2) * COLS :], own[: 2 * COLS])
    rows = lax.ppermute(to_row, "row", [(0, 1), (1, 0)])
    main1 = ahead(own, perm=next_frame)
    half_way = ahead(own, perm=backward(count, 0, HALF))
    to_core, to_far, held = pack(meta, own, rows)
    first_weight = bring(tie(conv1_weight, to_core))
    near = lax.ppermute(to_core, "col", [(0, 1), (1, 0), (2, 3), (3, 2)])
    far = lax.ppermute(to_far, "col", [(0, 3), (3, 0), (1, 2), (2, 1)])
    strips0 = join(tie(rows, first_weight), near, far)
    strips1 = ahead(strips0, perm=next_frame)
    strips2 = ahead(strips0, perm=shifted(count, 2))
    strips4 = ahead(strips0, perm=shifted(count, 4))

    main2 = ahead(tie(main1, to_core), perm=next_frame)
    main4 = ahead(half_way, perm=backward(count, HALF, 4 - HALF))
    biases = (conv1_bias.reshape(1, CH), conv2_bias.reshape(1, CH))
    weights = (first_weight, conv2_weight, biases)
    frames = [([held], strips0), ([main1], strips1)]
    sums, total = step(0, tie(meta, half_way), frames[:1], weights, held, {}, None)
    main2 = tie(main2, sums[0])
    main3 = ahead(main2, perm=next_frame)
    sums, total = step(1, meta, frames, weights, held, sums, total)
    strips3 = ahead(tie(strips2, sums[0]), perm=next_frame)
    frames += [([main2], strips2), ([main3], strips3), ([main4], strips4)]
    sums, total = step(2, meta, frames[:3], weights, held, sums, total)
    sums, total = step(4, meta, frames, weights, held, sums, total)
    out = step(3, meta, frames[:4], weights, held, sums, total)
    return out.reshape(1, ROWS, COLS, CH)


def solution(mesh):
    in_specs = (P("tm", "row", "col", None), P(), P(), P(), P())
    out_specs = P("tm", "row", "col", None)
    return jax.shard_map(local, mesh=mesh, in_specs=in_specs, out_specs=out_specs, check_vma=False)
```

```python
import functools

import jax
import jax.numpy as jnp
from jax import lax
from jax.experimental import pallas as pl
from jax.experimental.pallas import tpu as pltpu
from jax.sharding import PartitionSpec as P

RING = 8
CH = 256
ROWS, COLS = 45, 16
LIMIT = 30 * 2**20
COST = (1000000000, 2000000000, 2000000000, 3000000000, 500000000)
FORTH = (45,)
BACK = (45,)
HALF = 2
WIDE = 32
PR = ROWS + 3
HR = ROWS + 1
MAIN = HR * COLS
SIDE = PR
ACC = MAIN + 2 * SIDE
BF, F32 = jnp.bfloat16, jnp.float32


def shifted(count, steps):
    return [(i, (i + steps) % count) for i in range(count)]


def backward_place(source, steps, count):
    block, place = divmod(source, RING)
    early = 0 < steps < 4
    moved = place in ((4, 5, 6) if early else (4, 5, 6, 7)) if steps else False
    return ((block + moved) * RING + (place - steps) % RING) % count


def backward(count, done, steps):
    return [
        (backward_place(i, done, count), backward_place(i, done + steps, count))
        for i in range(count)
    ]


def silu(v):
    return (0.5 * v) * (1.0 + jnp.tanh(0.5 * v))


def rounded(v):
    return v.astype(BF).astype(F32)


def take(work, start, size, stride=None):
    return jnp.concatenate([work[h, pl.ds(start, size, stride), :] for h in range(2)], axis=1)


def put(work, start, size, value, stride=None):
    for h in range(2):
        work[h, pl.ds(start, size, stride), :] = value[:, h * 128 : (h + 1) * 128]


def pack_kernel(meta, main, halo, out_core, out_far, own, work):
    own[...] = main[...]
    row, col = meta[1], meta[2]
    first = 1 + row
    for r in range(ROWS):
        put(work, pl.multiple_of((first + r) * COLS, COLS), COLS, main[pl.ds(r * COLS, COLS), :].astype(F32))
    place = jnp.where(row == 0, ROWS + 1, 0)
    put(work, pl.multiple_of(place * COLS, COLS), 2 * COLS, halo[...].astype(F32))
    src = jnp.where(row == 0, 1, ROWS + 1)
    dst = jnp.where(row == 0, 0, ROWS + 2)
    edge = take(work, pl.multiple_of(src * COLS, COLS), COLS)
    put(work, pl.multiple_of(dst * COLS, COLS), COLS, edge)
    even = lax.rem(col, 2) == 0
    for i in range(2):
        left = take(work, i, PR, COLS)
        right = take(work, COLS - 2 + i, PR, COLS)
        out_core[pl.ds(i * PR, PR), :] = jnp.where(even, right, left).astype(BF)
        out_far[pl.ds(i * PR, PR), :] = jnp.where(even, left, right).astype(BF)


def shift_columns(work, x, rows):
    for r in range(rows):
        for kw in range(3):
            x[kw, pl.ds(r * COLS, COLS), :] = take(work, r * WIDE + 7 + kw, COLS).astype(BF)


def build_frame(meta, main, strips, work, edge, x, side):
    row, col = meta[1], meta[2]
    first = 1 + row
    for r in range(ROWS):
        v = rounded(silu(main[pl.ds(r * COLS, COLS), :].astype(F32)))
        put(work, pl.multiple_of((first + r) * WIDE + 8, 8), COLS, v)
    place = jnp.where(row == 0, ROWS + 1, 0)
    for r in range(2):
        v = rounded(silu(strips[pl.ds(r * COLS, COLS), :].astype(F32)))
        put(work, pl.multiple_of((place + r) * WIDE + 8, 8), COLS, v)
    src = jnp.where(row == 0, 1, ROWS + 1)
    dst = jnp.where(row == 0, 0, ROWS + 2)
    copied = take(work, pl.multiple_of(src * WIDE + 8, 8), COLS)
    put(work, pl.multiple_of(dst * WIDE + 8, 8), COLS, copied)
    even = lax.rem(col, 2) == 0
    west = take(work, 8, PR, WIDE)
    east = take(work, 8 + COLS - 1, PR, WIDE)
    for i in range(2):
        near = rounded(silu(strips[pl.ds(2 * COLS + i * PR, PR), :].astype(F32)))
        far = rounded(silu(strips[pl.ds(2 * COLS + (2 + i) * PR, PR), :].astype(F32)))
        left = jnp.where(col == 0, west, jnp.where(even, far, near))
        right = jnp.where(col == 3, east, jnp.where(even, near, far))
        put(work, 6 + i, PR, left, WIDE)
        put(work, 8 + COLS + i, PR, right, WIDE)
        edge[i, pl.ds(0, PR), :] = left
        edge[4 + i, pl.ds(0, PR), :] = right
    edge[2, pl.ds(0, PR), :] = west
    edge[3, pl.ds(0, PR), :] = east
    for c in range(6):
        edge[c, pl.ds(PR, 8), :] = jnp.zeros((8, CH), F32)
    shift_columns(work, x, PR)
    for kh in range(3):
        for s in range(2):
            for kw in range(3):
                side[kh, kw, pl.ds(s * SIDE, SIDE), :] = edge[3 * s + kw, pl.ds(kh, SIDE), :].astype(BF)


def first_taps(x, side, weight, carried, out):
    cells = jnp.concatenate(
        [
            jnp.concatenate([x[kw, pl.ds(kh * COLS, MAIN), :], side[kh, kw]], axis=0)
            for kh in range(3)
            for kw in range(3)
        ],
        axis=1,
    )
    part = jnp.dot(cells, weight.reshape(9 * CH, CH), preferred_element_type=F32)
    out[...] = part if carried is None else carried[...] + part


def second_taps(x, weight):
    cells = jnp.concatenate(
        [x[kw, pl.ds(kh * COLS, ROWS * COLS), :] for kh in range(3) for kw in range(3)], axis=1
    )
    return jnp.dot(cells, weight.reshape(9 * CH, CH), preferred_element_type=F32)


def build_hidden(meta, acc, bias, work, x):
    row, col = meta[1], meta[2]
    first = 1 - row
    b = bias
    for r in range(HR):
        v = rounded(silu(acc[pl.ds(r * COLS, COLS), :] + b))
        put(work, pl.multiple_of((first + r) * WIDE + 8, 8), COLS, v)
    left = rounded(silu(acc[pl.ds(MAIN, HR), :] + b))
    right = rounded(silu(acc[pl.ds(MAIN + SIDE, HR), :] + b))
    for edge_row, start in ((0, 1), (1, 0)):

        @pl.when(row == edge_row)
        def _():
            west = take(work, start * WIDE + 8, HR, WIDE)
            east = take(work, start * WIDE + 8 + COLS - 1, HR, WIDE)
            put(work, start * WIDE + 7, HR, jnp.where(col == 0, west, left), WIDE)
            put(work, start * WIDE + 8 + COLS, HR, jnp.where(col == 3, east, right), WIDE)
            src = 1 if edge_row == 0 else HR - 1
            dst = 0 if edge_row == 0 else HR
            put(work, dst * WIDE, WIDE, take(work, src * WIDE, WIDE))

    shift_columns(work, x, HR + 1)


def step_kernel(steps, plan, *refs):
    refs = list(refs)
    pop = lambda count: [refs.pop(0) for _ in range(count)]
    (meta,) = pop(1)
    mains = [pop(count) for count in plan["parts"]]
    strips = pop(steps + 1 - plan["late"])
    (w1,) = pop(1)
    w2, bias1 = pop(2) if plan["done"] else (None, None)
    bias2, latent = pop(2) if plan["last"] else (None, None)
    sums_in = dict(zip(plan["carried"], pop(len(plan["carried"]))))
    total_in = pop(1)[0] if plan["total_in"] else None
    outs = pop(plan["outs"])
    main, strip, work, edge, x, side, ready = refs[:7]
    for k in range(steps + 1):
        if plan["late"] and k == steps - 1:
            continue
        source = k - (plan["late"] and k == steps)

        @pl.when(meta[0] >= steps if k == steps else meta[0] == k)
        def _():
            main[...] = mains[source][0][...]
            strip[...] = strips[source][...]

    def add():
        build_frame(meta, main, strip, work, edge, x, side)
        kept = [f for f in plan["frames"] if f not in plan["done"]]
        for frame in plan["frames"][::-1]:
            if frame in plan["done"]:
                out = ready.at[plan["done"].index(frame)]
            else:
                out = outs[kept.index(frame)]
            first_taps(x, side, w1[2 - (steps - frame)], sums_in.get(frame), out)

    if plan["late"]:
        pl.when(meta[0] != steps - 1)(add)

        @pl.when(meta[0] == steps - 1)
        def _():
            outs[0][...] = sums_in[plan["frames"][0]][...]

    else:
        add()
    if plan["last"]:

        @pl.when(meta[0] == steps)
        def _():
            first_taps(x, side, w1[0], ready.at[1], ready.at[1])

    if plan["done"]:
        total = 0.0 if total_in is None else total_in[...]
        for i, frame in enumerate(plan["done"]):
            room = (work, x) if i == 0 else refs[7:9]
            build_hidden(meta, ready.at[i], bias1[...], *room)
        for i, frame in enumerate(plan["done"]):
            total = total + second_taps(x if i == 0 else refs[8], w2[2 - frame])
        if plan["last"]:
            total = (latent[...].astype(F32) + (total + bias2[...])).astype(BF)
        outs[-1][...] = total


SCRATCH = [
    pltpu.VMEM((ROWS * COLS, CH), BF),
    pltpu.VMEM((2 * COLS + 4 * PR, CH), BF),
    pltpu.VMEM((2, PR * WIDE, 128), F32),
    pltpu.VMEM((6, PR + 8, CH), F32),
    pltpu.VMEM((3, PR * COLS, CH), BF),
    pltpu.VMEM((3, 3, 2 * SIDE, CH), BF),
    pltpu.VMEM((2, ACC, CH), F32),
]
SECOND = [
    pltpu.VMEM((2, PR * WIDE, 128), F32),
    pltpu.VMEM((3, PR * COLS, CH), BF),
]
ANY = pl.BlockSpec(memory_space=pl.ANY)
SMEM = pl.BlockSpec(memory_space=pltpu.SMEM)
VMEM = pl.BlockSpec(memory_space=pltpu.VMEM)


def step(steps, meta, frames, weights, latent, sums, total):
    late = steps == 4
    last = steps == 3
    frames_here = [f for f in range(3) if 0 <= steps - f <= 2]
    done = {2: [0], 3: [1, 2]}.get(steps, [])
    if late:
        frames = frames[:3] + frames[4:]
    plan = {
        "frames": frames_here,
        "carried": [f for f in frames_here if f in sums],
        "done": done,
        "last": last,
        "late": late,
        "total_in": total is not None and not late,
    }
    hid = jax.ShapeDtypeStruct((ACC, CH), F32)
    tot = jax.ShapeDtypeStruct((ROWS * COLS, CH), F32)
    kept = [f for f in frames_here if f not in done]
    out_shape = [hid] * len(kept)
    if last:
        out_shape = [jax.ShapeDtypeStruct((ROWS * COLS, CH), BF)]
    elif done:
        out_shape = out_shape + [tot]
    plan["outs"] = len(out_shape)
    mains = [part for f in frames for part in f[0]]
    strips = [f[1] for f in frames if f[1] is not None]
    plan["parts"] = [len(f[0]) for f in frames]
    w1, w2, biases = weights
    args = [meta, *mains, *strips, w1]
    args += [w2, biases[0]] if done else []
    args += [biases[1], latent] if last else []
    args += [sums[f] for f in plan["carried"]] + ([total] if plan["total_in"] else [])
    specs = [SMEM] + [VMEM] * (len(args) - 1)
    outs = pl.pallas_call(
        functools.partial(step_kernel, steps, plan),
        out_shape=out_shape,
        in_specs=specs,
        out_specs=[VMEM] * len(out_shape),
        scratch_shapes=SCRATCH + (SECOND if last else []),
        compiler_params=pltpu.CompilerParams(vmem_limit_bytes=LIMIT),
        cost_estimate=pl.CostEstimate(
            flops=COST[steps],
            bytes_accessed=1000000,
            transcendentals=0,
        ),
        name="step" + str(steps),
    )(*args)
    if last:
        return outs[0]
    return {**sums, **dict(zip(kept, outs))}, (outs[-1] if done else total)


def bring_kernel(source, target, sem):
    copy = pltpu.make_async_copy(source, target, sem)
    copy.start()
    copy.wait()


def bring(weight):
    return pl.pallas_call(
        bring_kernel,
        out_shape=jax.ShapeDtypeStruct(weight.shape, weight.dtype),
        in_specs=[ANY],
        out_specs=VMEM,
        scratch_shapes=[pltpu.SemaphoreType.DMA],
        compiler_params=pltpu.CompilerParams(vmem_limit_bytes=LIMIT),
        cost_estimate=pl.CostEstimate(flops=1000000000, bytes_accessed=1000, transcendentals=0),
        name="bring",
    )(weight)


def tie(value, *first):
    return lax.optimization_barrier((value, *first))[0]


def join_kernel(*refs):
    *parts, out = refs
    at = 0
    for part in parts:
        out[pl.ds(at, part.shape[0]), :] = part[...]
        at += part.shape[0]


def join(*parts):
    return pl.pallas_call(
        join_kernel,
        out_shape=jax.ShapeDtypeStruct((sum(p.shape[0] for p in parts), CH), BF),
        in_specs=[VMEM] * len(parts),
        out_specs=VMEM,
        compiler_params=pltpu.CompilerParams(vmem_limit_bytes=LIMIT),
        cost_estimate=pl.CostEstimate(flops=1000000, bytes_accessed=800000, transcendentals=0),
        name="join",
    )(*parts)


def cut_kernel(meta, own, to_row, *parts):
    last = ROWS - 2
    to_row[...] = jnp.where(
        meta[1] == 0, own[pl.ds(last * COLS, 2 * COLS), :], own[pl.ds(0, 2 * COLS), :]
    )
    at = 0
    for part in parts:
        if at == ROWS * COLS:
            at = 0
        part[...] = own[pl.ds(at, part.shape[0]), :]
        at += part.shape[0]


def cut(meta, own, sizes):
    shapes = [jax.ShapeDtypeStruct((r * COLS, CH), BF) for r in (2, *sizes)]
    return pl.pallas_call(
        cut_kernel,
        out_shape=shapes,
        in_specs=[SMEM, VMEM],
        out_specs=[VMEM] * len(shapes),
        compiler_params=pltpu.CompilerParams(vmem_limit_bytes=LIMIT),
        cost_estimate=pl.CostEstimate(flops=1000000, bytes_accessed=800000, transcendentals=0),
        name="cut",
    )(meta, own)


def pack(meta, own, rows):
    edge = jax.ShapeDtypeStruct((2 * PR, CH), BF)
    return pl.pallas_call(
        pack_kernel,
        out_shape=[
            edge,
            edge,
            jax.ShapeDtypeStruct((ROWS * COLS, CH), BF),
        ],
        in_specs=[SMEM, VMEM, VMEM],
        out_specs=[VMEM] * 3,
        scratch_shapes=[pltpu.VMEM((2, PR * COLS, 128), F32)],
        compiler_params=pltpu.CompilerParams(vmem_limit_bytes=LIMIT),
        cost_estimate=pl.CostEstimate(flops=1000000, bytes_accessed=800000, transcendentals=0),
        name="pack",
    )(meta, own, rows)


def local(latent, conv1_weight, conv1_bias, conv2_weight, conv2_bias):
    count = lax.axis_size("tm")
    t = lax.axis_index("tm").astype(jnp.int32)
    row = lax.axis_index("row").astype(jnp.int32)
    col = lax.axis_index("col").astype(jnp.int32)
    meta = jnp.stack([t, row, col])
    own = latent.reshape(ROWS * COLS, CH)

    ahead = functools.partial(lax.ppermute, axis_name="tm")
    next_frame = shifted(count, 1)
    to_row = jnp.where(row == 0, own[(ROWS - 2) * COLS :], own[: 2 * COLS])
    rows = lax.ppermute(to_row, "row", [(0, 1), (1, 0)])
    main1 = ahead(own, perm=next_frame)
    half_way = ahead(own, perm=backward(count, 0, HALF))
    to_core, to_far, held = pack(meta, own, rows)
    first_weight = bring(tie(conv1_weight, to_core))
    near = lax.ppermute(to_core, "col", [(0, 1), (1, 0), (2, 3), (3, 2)])
    far = lax.ppermute(to_far, "col", [(0, 3), (3, 0), (1, 2), (2, 1)])
    strips0 = join(tie(rows, first_weight), near, far)
    strips1 = ahead(strips0, perm=next_frame)
    strips2 = ahead(strips0, perm=shifted(count, 2))

    main2 = ahead(tie(main1, to_core), perm=next_frame)
    main4 = ahead(half_way, perm=backward(count, HALF, 4 - HALF))
    biases = (conv1_bias.reshape(1, CH), conv2_bias.reshape(1, CH))
    weights = (first_weight, conv2_weight, biases)
    frames = [([held], strips0), ([main1], strips1)]
    sums, total = step(0, tie(meta, half_way), frames[:1], weights, held, {}, None)
    main2 = tie(main2, sums[0])
    main3 = ahead(main2, perm=next_frame)
    sums, total = step(1, meta, frames, weights, held, sums, total)
    strips3 = ahead(tie(strips2, sums[0]), perm=next_frame)
    strips4 = ahead(tie(strips2, sums[0]), perm=shifted(count, 2))
    frames += [([main2], strips2), ([main3], strips3), ([main4], strips4)]
    sums, total = step(2, meta, frames[:3], weights, held, sums, total)
    sums, total = step(4, meta, frames, weights, held, sums, total)
    out = step(3, meta, frames[:4], weights, held, sums, total)
    return out.reshape(1, ROWS, COLS, CH)


def solution(mesh):
    in_specs = (P("tm", "row", "col", None), P(), P(), P(), P())
    out_specs = P("tm", "row", "col", None)
    return jax.shard_map(local, mesh=mesh, in_specs=in_specs, out_specs=out_specs, check_vma=False)
```
